32 devices in a mesh: parts: 2 (over y), tp: 16 (over z, x, core).
Axes of the slice: x: 2, y: 2, z: 4, core: 2. Of those that a mesh axis runs over, the one named last changes fastest.
Arguments:
- inputs: bfloat16 [512, 5120], P(('parts', 'tp')), parts along dimension 0, may hold values from -6 to 6
- out_grads: bfloat16 [2, 512, 25600], P(None, 'parts', 'tp'), parts along dimension 1, may hold values from -6 to 6
- frozen_weights: bfloat16 [2, 25600, 5120], P(None, 'tp'), may hold values from -0.078125 to 0.078125
- adapter_first: bfloat16 [2, 512, 5120], P(None, ('parts', 'tp')), parts along dimension 1, may hold values from -0.078125 to 0.078125
- adapter_second: bfloat16 [2, 512, 25600], P(None, ('parts', 'tp')), parts along dimension 1, may hold values from -0.3125 to 0.3125
- group_jobs: int32 [8], P('parts'), parts along dimension 0, may hold values from 0 to 3, each once
- owner_map: int32 [32], P('parts'), parts along dimension 0, may hold values from 0 to 15, each once
- segment_offsets: int32 [10], P('parts'), parts along dimension 0, may hold values from 0 to 256, as said below
- segment_lengths: int32 [8], P('parts'), parts along dimension 0, may hold values from 1 to 120, as said below
Outputs:
- input_grads: float32 [512, 5120], P(('parts', 'tp')), parts along dimension 0
- first_factor_gradient: float32 [2, 512, 5120], P(None, ('parts', 'tp')), parts along dimension 1
- second_factor_gradient: float32 [2, 512, 25600], P(None, ('parts', 'tp')), parts along dimension 1
The draws below stay inside these ranges and needn't reach their ends.
There are 2 independent parts, one for each index of `parts`. The reference program is written for one: setup_inputs(seed, part) draws one part's arguments, and reference() takes and returns one part's arrays. A program takes and returns all parts, laid end to end along the dimension named above; an argument that names none is the same for every part. Nothing has to cross between parts.
Inputs may be any that keep to these rules, and one draw needn't show every extreme that they name: `group_jobs`: every job appears in exactly one slot. Device owner_map[j * 4 + q] stores rank rows q * 16 to (q + 1) * 16 - 1 of job j, at its local rows in that order; every device stores one piece. `segment_offsets`: starts at 0, rises strictly in multiples of 8, the last entry is 256. Slot s has segment_lengths[s] live tokens from segment_offsets[s] on; fewer than 8 positions of its padded span are padding. One slot in every draw has the largest length, with no padding.
All inputs are finite; a program needn't handle non-finite values.
Results may differ from the reference program's by a relative error of at most 0.003.
Values may be sent and summed in bfloat16 or wider, within the bound.
A program may use at most 192 MiB of HBM per device.

```python
import jax
import jax.numpy as jnp
from jax import lax

MODEL_WIDTH = 5120
FF = 25600
R = 64
SPLIT = 4
BLK = 8
PACKED_TOKENS = 256
ADAPTER_JOBS = 4
N_TP = 16


def segment_plan(key):
    blocks = PACKED_TOKENS // BLK
    big_blocks = (blocks - ADAPTER_JOBS + 3) // 2
    rest_blocks = blocks - big_blocks
    cut_key = jax.random.fold_in(key, 21)
    short_key = jax.random.fold_in(key, 22)
    place_key = jax.random.fold_in(key, 23)
    cuts = jnp.sort(jax.random.permutation(cut_key, rest_blocks - 1)[:ADAPTER_JOBS - 2] + 1).astype(jnp.int32)
    bounds = jnp.concatenate([jnp.zeros((1,), jnp.int32), cuts, jnp.full((1,), rest_blocks, jnp.int32)])
    rest_spans = bounds[1:] - bounds[:-1]
    big_slot = jax.random.randint(place_key, (), 0, ADAPTER_JOBS, dtype=jnp.int32)
    slot_ids = jnp.arange(ADAPTER_JOBS, dtype=jnp.int32)
    before = rest_spans[jnp.clip(slot_ids, 0, ADAPTER_JOBS - 2)]
    after = rest_spans[jnp.clip(slot_ids - 1, 0, ADAPTER_JOBS - 2)]
    block_spans = jnp.where(slot_ids < big_slot, before, jnp.where(slot_ids == big_slot, big_blocks, after)).astype(jnp.int32)
    spans = block_spans * BLK
    offsets = jnp.concatenate([jnp.zeros((1,), jnp.int32), jnp.cumsum(spans).astype(jnp.int32)])
    shortfall = jax.random.randint(short_key, (ADAPTER_JOBS,), 0, BLK, dtype=jnp.int32)
    shortfall = jnp.where(slot_ids == big_slot, 0, shortfall)
    return (offsets, (spans - shortfall).astype(jnp.int32))


def draw_segment_offsets(key, part):
    offsets, lengths = segment_plan(key)
    return offsets


def draw_segment_lengths(key, part):
    offsets, lengths = segment_plan(key)
    return lengths


def raised(values, rng, source, target, parts, factor):
    def block_of(position):
        return (jnp.arange(values.shape[position]) // (values.shape[position] // parts)).reshape((-1,) + (1,) * (values.ndim - 1 - position))

    one_side = jax.random.permutation(rng, parts)[block_of(target)]
    other_side = (block_of(target) + parts // 2) % parts
    return jnp.where((block_of(source) == one_side) | (block_of(source) == other_side), factor * values, values)


def shard_levels(key, extent, cuts, low, top_value):
    level, own = 1.0, jax.random.fold_in(key, 6)
    for dim, parts in cuts:
        steps = jnp.exp(jax.random.uniform(jax.random.fold_in(own, dim), (parts,), jnp.float32, low / len(cuts), top_value / len(cuts)))
        level = level * jnp.repeat(steps, extent[dim] // parts).reshape([-1 if axis == dim else 1 for axis in range(len(extent))])
    return level


def normal_values(rng, shape, scale, bound, shards=(), kind=jnp.bfloat16):
    loudness = shard_levels(rng, shape, shards, -0.22, 0.18) if shards else 1.0
    result = jax.random.normal(rng, shape, jnp.float32) * scale * loudness
    return jnp.minimum(jnp.maximum(result, -bound), bound).astype(kind)


def noise_with(own_key, dims, spread, limit, cuts, heavy, held_as=jnp.bfloat16):
    array = spread * jax.random.normal(own_key, dims, jnp.float32)
    if cuts:
        array = array * shard_levels(own_key, dims, cuts, -0.22, 0.18)
    return jnp.clip(raised(array, jax.random.fold_in(own_key, 3), *heavy), -limit, limit).astype(held_as)


def setup_inputs(seed: int = 0, part: int = 0) -> dict:
    keys = jax.random.split(jax.random.key(seed), 10)
    own_keys = jax.random.split(jax.random.fold_in(keys[9], part), 10)
    return {
        "inputs": normal_values(own_keys[0], (PACKED_TOKENS, MODEL_WIDTH), 1.0, 6.0, ((0, 16),)),
        "out_grads": noise_with(own_keys[1], (2, PACKED_TOKENS, FF), 1.0, 6.0, ((2, 16),), (2, 1, 16, 2.0)),
        "frozen_weights": normal_values(keys[2], (2, FF, MODEL_WIDTH), MODEL_WIDTH ** -0.5, 0.078125, ((1, 16),)),
        "adapter_first": normal_values(own_keys[3], (2, ADAPTER_JOBS * R, MODEL_WIDTH), MODEL_WIDTH ** -0.5, 0.078125, ((1, 16),)),
        "adapter_second": normal_values(own_keys[4], (2, ADAPTER_JOBS * R, FF), (FF // 64) ** -0.5, 0.3125, ((1, 16),)),
        "group_jobs": jax.random.permutation(own_keys[5], ADAPTER_JOBS).astype(jnp.int32),
        "owner_map": jax.random.permutation(own_keys[6], N_TP).astype(jnp.int32),
        "segment_offsets": draw_segment_offsets(jax.random.fold_in(jax.random.fold_in(keys[9], part), 71), part),
        "segment_lengths": draw_segment_lengths(jax.random.fold_in(jax.random.fold_in(keys[9], part), 71), part),
    }


adapter_scale = 0.5


def token_tables(segment_offsets, segment_lengths):
    positions = jnp.arange(PACKED_TOKENS, dtype=jnp.int32)
    slot_ids = jnp.arange(ADAPTER_JOBS, dtype=jnp.int32)
    slot_of = jnp.sum((positions[:, None] >= segment_offsets[1:ADAPTER_JOBS][None, :]).astype(jnp.int32), axis=1)
    onehot = slot_of[:, None] == slot_ids[None, :]
    starts = jnp.sum(jnp.where(onehot, segment_offsets[:ADAPTER_JOBS][None, :], 0), axis=1)
    spans = jnp.sum(jnp.where(onehot, segment_lengths[None, :], 0), axis=1)
    live_mask = positions - starts < spans
    return slot_of, live_mask


def adapter_rows(group_jobs, owner_map):
    piece_rows = R // SPLIT
    pieces = owner_map.reshape(ADAPTER_JOBS, SPLIT)[group_jobs]
    within = jnp.arange(piece_rows, dtype=jnp.int32)
    return (pieces[:, :, None] * piece_rows + within[None, None, :]).reshape(ADAPTER_JOBS, R)


def narrowed(values):
    rounded = lax.optimization_barrier(values.astype(jnp.bfloat16))
    return rounded.astype(jnp.float32)


def reference(inputs, out_grads, frozen_weights, adapter_first, adapter_second, group_jobs, owner_map, segment_offsets, segment_lengths):
    slot_of, live_mask = token_tables(segment_offsets, segment_lengths)
    masked = out_grads * live_mask[None, :, None].astype(out_grads.dtype)
    masked_width_rows = masked.astype(jnp.float32)
    input_width_rows = inputs.astype(jnp.float32)
    rows_index = adapter_rows(group_jobs, owner_map)
    frozen_product = jnp.dot(masked[0], frozen_weights[0], preferred_element_type=jnp.float32)
    frozen_product = frozen_product + jnp.dot(masked[1], frozen_weights[1], preferred_element_type=jnp.float32)

    def slot_entries(adapter_gradients, slot_number):
        rows = rows_index[slot_number]
        first_factor_rows = jnp.take(adapter_first, rows, axis=1).astype(jnp.float32)
        second_rows = jnp.take(adapter_second, rows, axis=1).astype(jnp.float32)
        in_slot = (slot_of == slot_number).astype(jnp.float32)[None, :, None]
        rank_projection = narrowed(jnp.einsum("td,prd->ptr", input_width_rows, first_factor_rows) * in_slot)
        rank_backward = narrowed(jnp.einsum("ptf,prf->ptr", masked_width_rows, second_rows) * in_slot)
        adapter_gradients = adapter_gradients + adapter_scale * jnp.einsum("yjw,ywq->jq", rank_backward, first_factor_rows)
        first_gradient_rows = adapter_scale * jnp.einsum("vyc,ys->vcs", rank_backward, input_width_rows)
        second_gradient_rows = adapter_scale * jnp.einsum("byu,byc->buc", rank_projection, masked_width_rows)
        return adapter_gradients, (first_gradient_rows, second_gradient_rows)

    adapter_product, stacked_gradients = lax.scan(slot_entries, jnp.zeros((PACKED_TOKENS, MODEL_WIDTH), jnp.float32), jnp.arange(ADAPTER_JOBS, dtype=jnp.int32))
    grads_first, grads_second = stacked_gradients
    flat_rows = rows_index.reshape(-1)
    ordered_first = jnp.transpose(grads_first, (1, 0, 2, 3)).reshape(2, ADAPTER_JOBS * R, MODEL_WIDTH)
    ordered_second = jnp.transpose(grads_second, (1, 0, 2, 3)).reshape(2, ADAPTER_JOBS * R, FF)
    first_factor_gradient = jnp.zeros((2, ADAPTER_JOBS * R, MODEL_WIDTH), jnp.float32).at[:, flat_rows].set(ordered_first)
    second_factor_gradient = jnp.zeros((2, ADAPTER_JOBS * R, FF), jnp.float32).at[:, flat_rows].set(ordered_second)
    return (frozen_product + adapter_product, first_factor_gradient, second_factor_gradient)
```

```python
import functools

import jax
import jax.numpy as jnp
from jax import lax
from jax.experimental import pallas as pl
from jax.experimental.pallas import tpu as pltpu
from jax.sharding import PartitionSpec as P

R = 64
SPLIT = 4
adapter_scale = 0.5
PARAMS = pltpu.CompilerParams(vmem_limit_bytes=48 * 1024 * 1024)
f32 = jnp.float32
bf16 = jnp.bfloat16


def pack_kernel(tp, hidden, width, second_ref, first_ref, inputs_ref, out_ref):
    piece, tok, half = first_ref.shape[1], inputs_ref.shape[0], width // 2
    at = hidden + width
    for d in range(tp):
        for p in range(2):
            rows = slice(p * piece, (p + 1) * piece)
            out_ref[d, rows, :hidden] = second_ref[p, :, d * hidden : (d + 1) * hidden]
            out_ref[d, rows, hidden:at] = first_ref[p, :, d * width : (d + 1) * width]
            start = d * width + p * half
            out_ref[d, p * piece : p * piece + tok, at:] = inputs_ref[:, start : start + half]


def contract(a, b, dims, precision=None):
    return lax.dot_general(a, b, (dims, ((), ())), precision=precision, preferred_element_type=f32)


def project_kernel(
    tp, hidden, width, piece, tok, got_ref, grads_ref, live_ref, match_ref, pick_ref, out_ref, cols_ref, x_ref
):
    half, at = width // 2, hidden + width
    for d in range(tp):
        for p in range(2):
            x_ref[d * tok : (d + 1) * tok, p * half : (p + 1) * half] = got_ref[
                d, p * piece : p * piece + tok, at:
            ].astype(f32)
    x = x_ref[...].astype(bf16)
    cols_ref[...] = x
    match = match_ref[...]
    pick = pick_ref[...]
    live = live_ref[...]
    for p in range(2):
        rows = slice(p * piece, (p + 1) * piece)
        first = got_ref[:, rows, hidden:at].reshape(tp * piece, width)
        second = got_ref[:, rows, :hidden].reshape(tp * piece, hidden)
        low = contract(x, first, ((1,), (1,)))
        back = contract(grads_ref[p] * live, second, ((1,), (1,)))
        for k, value in ((p, low), (2 + p, back)):
            kept = jnp.where(match > 0, value, 0.0)
            out_ref[:, k * R : (k + 1) * R] = contract(
                kept, pick, ((1,), (0,)), precision=lax.Precision.HIGHEST
            )


def gradient_kernel(
    tp, hidden, width, piece, tok, got_ref, grads_ref, live_ref, match_ref, pick_ref, cols_ref, rank_ref, out_ref, a_ref
):
    half, at = width // 2, hidden + width
    match = match_ref[...]
    pick = pick_ref[...].astype(bf16)
    live = live_ref[...]
    x = cols_ref[...]
    total = None
    for p in range(2):
        rows = slice(p * piece, (p + 1) * piece)

        def spread(k):
            wide = contract(rank_ref[:, k * R : (k + 1) * R], pick, ((1,), (1,)))
            return jnp.where(match > 0, wide, 0.0).astype(bf16)

        low, back = spread(p), spread(2 + p)
        first = got_ref[:, rows, hidden:at].reshape(tp * piece, width)
        term = contract(back, first, ((1,), (0,)))
        total = term if total is None else total + term
        first_gradient = adapter_scale * contract(back, x, ((0,), (0,)))
        out_ref[:, rows, hidden:at] = first_gradient.astype(bf16).reshape(tp, piece, width)
        second_gradient = adapter_scale * contract(low, grads_ref[p] * live, ((0,), (0,)))
        out_ref[:, rows, :hidden] = second_gradient.astype(bf16).reshape(tp, piece, hidden)
    a_ref[...] = adapter_scale * total
    for d in range(tp):
        for p in range(2):
            out_ref[d, p * piece : p * piece + tok, at:] = a_ref[
                d * tok : (d + 1) * tok, p * half : (p + 1) * half
            ].astype(bf16)


def unpack_kernel(tp, hidden, width, got_ref, base_ref, grads_ref, first_ref, second_ref):
    piece, tok, half = first_ref.shape[1], base_ref.shape[0], width // 2
    at = hidden + width
    for d in range(tp):
        for p in range(2):
            rows = slice(p * piece, (p + 1) * piece)
            second_ref[p, :, d * hidden : (d + 1) * hidden] = got_ref[d, rows, :hidden].astype(f32)
            first_ref[p, :, d * width : (d + 1) * width] = got_ref[d, rows, hidden:at].astype(f32)
            cut = slice(d * width + p * half, d * width + (p + 1) * half)
            grads_ref[:, cut] = base_ref[:, cut] + got_ref[d, p * piece : p * piece + tok, at:].astype(f32)


def shards(
    inputs,
    out_grads,
    frozen_weights,
    adapter_first,
    adapter_second,
    group_jobs,
    owner_map,
    segment_offsets,
    segment_lengths,
):
    tp = lax.axis_size("tp")
    job_count = group_jobs.shape[0]
    tokens, hidden = out_grads.shape[1:]
    tok, model = inputs.shape
    width = model // tp
    piece = adapter_first.shape[1]
    total_rows = tp * piece
    wide = hidden + width + width // 2
    sizes = (tp, hidden, width)

    packed = pl.pallas_call(
        functools.partial(pack_kernel, *sizes),
        out_shape=jax.ShapeDtypeStruct((tp, 2 * piece, wide), bf16),
        compiler_params=PARAMS,
    )(adapter_second, adapter_first, inputs)
    got = lax.all_to_all(packed, "tp", split_axis=0, concat_axis=0, tiled=True)

    positions = jnp.arange(tokens, dtype=jnp.int32)
    slot_ids = jnp.arange(job_count, dtype=jnp.int32)
    slot_of = jnp.sum((positions[:, None] >= segment_offsets[1:job_count][None, :]).astype(jnp.int32), axis=1)
    onehot = slot_of[:, None] == slot_ids[None, :]
    starts = jnp.sum(jnp.where(onehot, segment_offsets[:job_count][None, :], 0), axis=1)
    spans = jnp.sum(jnp.where(onehot, segment_lengths[None, :], 0), axis=1)
    live = (positions - starts < spans).astype(out_grads.dtype)[:, None]
    row = jnp.arange(total_rows, dtype=jnp.int32)
    entries = jnp.arange(tp, dtype=jnp.int32)
    entry = jnp.sum(jnp.where(owner_map[None, :] == (row // piece)[:, None], entries[None, :], 0), axis=1)
    row_slot = jnp.sum(
        jnp.where(group_jobs[None, :] == (entry // SPLIT)[:, None], slot_ids[None, :], 0), axis=1
    )
    rank = (entry % SPLIT) * piece + row % piece
    match = (slot_of[:, None] == row_slot[None, :]).astype(f32)
    pick = (rank[:, None] == jnp.arange(R, dtype=jnp.int32)[None, :]).astype(f32)

    masked = out_grads * live[None]
    frozen_product = jnp.einsum("ptf,pfd->td", masked, frozen_weights, preferred_element_type=f32)
    frozen_rows = lax.psum_scatter(frozen_product, "tp", scatter_dimension=0, tiled=True)

    parts, columns = pl.pallas_call(
        functools.partial(project_kernel, *sizes, piece, tok),
        out_shape=(
            jax.ShapeDtypeStruct((tokens, 4 * R), f32),
            jax.ShapeDtypeStruct((tokens, width), bf16),
        ),
        scratch_shapes=[pltpu.VMEM((tokens, width), f32)],
        compiler_params=PARAMS,
    )(got, out_grads, live, match, pick)
    swapped = lax.all_to_all(parts.reshape(tp, tok, 4 * R), "tp", split_axis=0, concat_axis=0, tiled=True)
    own_rank = jnp.sum(swapped, axis=0).astype(bf16)
    rank_values = lax.all_gather(own_rank, "tp", axis=0, tiled=True)

    outgoing = pl.pallas_call(
        functools.partial(gradient_kernel, *sizes, piece, tok),
        out_shape=jax.ShapeDtypeStruct((tp, 2 * piece, wide), bf16),
        scratch_shapes=[pltpu.VMEM((tokens, width), f32)],
        compiler_params=PARAMS,
    )(got, out_grads, live, match, pick, columns, rank_values)
    returned = lax.all_to_all(outgoing, "tp", split_axis=0, concat_axis=0, tiled=True)
    return pl.pallas_call(
        functools.partial(unpack_kernel, *sizes),
        out_shape=(
            jax.ShapeDtypeStruct((tok, model), f32),
            jax.ShapeDtypeStruct((2, piece, model), f32),
            jax.ShapeDtypeStruct((2, piece, tp * hidden), f32),
        ),
        compiler_params=PARAMS,
    )(returned, frozen_rows)


def solution(mesh):
    return jax.shard_map(
        shards,
        mesh=mesh,
        in_specs=(
            P(("parts", "tp"), None),
            P(None, "parts", "tp"),
            P(None, "tp", None),
            P(None, ("parts", "tp"), None),
            P(None, ("parts", "tp"), None),
            P("parts"),
            P("parts"),
            P("parts"),
            P("parts"),
        ),
        out_specs=(
            P(("parts", "tp"), None),
            P(None, ("parts", "tp"), None),
            P(None, ("parts", "tp"), None),
        ),
        check_vma=False,
    )
```

```python
import functools

import jax
import jax.numpy as jnp
from jax import lax
from jax.experimental import pallas as pl
from jax.experimental.pallas import tpu as pltpu
from jax.sharding import PartitionSpec as P

R = 64
SPLIT = 4
adapter_scale = 0.5
PARAMS = pltpu.CompilerParams(vmem_limit_bytes=48 * 1024 * 1024)
f32 = jnp.float32
bf16 = jnp.bfloat16


def pack_kernel(tp, hidden, width, second_ref, first_ref, inputs_ref, out_ref):
    piece, tok, half = first_ref.shape[1], inputs_ref.shape[0], width // 2
    at = hidden + width
    for d in range(tp):
        for p in range(2):
            rows = slice(p * piece, (p + 1) * piece)
            out_ref[d, rows, :hidden] = second_ref[p, :, d * hidden : (d + 1) * hidden]
            out_ref[d, rows, hidden:at] = first_ref[p, :, d * width : (d + 1) * width]
            start = d * width + p * half
            out_ref[d, p * piece : p * piece + tok, at:] = inputs_ref[:, start : start + half]


def contract(a, b, dims, precision=None):
    return lax.dot_general(a, b, (dims, ((), ())), precision=precision, preferred_element_type=f32)


def middle_kernel(
    tp, hidden, width, piece, tok, got_ref, grads_ref, live_ref, match_ref, pick_ref, out_ref,
    x_ref, flat_ref, parts_ref, landed_ref, rank_ref, sent_parts, came_parts, sent_rank, came_rank,
):
    half, at = width // 2, hidden + width
    me = lax.axis_index("tp")

    barrier = pltpu.get_barrier_semaphore()

    def greet(k, carry):
        pl.semaphore_signal(
            barrier, inc=1, device_id={"tp": lax.rem(me + k, tp)}, device_id_type=pl.DeviceIdType.MESH
        )
        return carry

    lax.fori_loop(1, tp, greet, 0)

    for d in range(tp):
        for p in range(2):
            x_ref[d * tok : (d + 1) * tok, p * half : (p + 1) * half] = got_ref[
                d, p * piece : p * piece + tok, at:
            ].astype(f32)
    x = x_ref[...].astype(bf16)
    match = match_ref[...]
    pick = pick_ref[...]
    live = live_ref[...]
    for p in range(2):
        rows = slice(p * piece, (p + 1) * piece)
        first = got_ref[:, rows, hidden:at].reshape(tp * piece, width)
        second = got_ref[:, rows, :hidden].reshape(tp * piece, hidden)
        low = contract(x, first, ((1,), (1,)))
        back = contract(grads_ref[p] * live, second, ((1,), (1,)))
        for k, value in ((p, low), (2 + p, back)):
            kept = jnp.where(match > 0, value, 0.0)
            flat_ref[:, k * R : (k + 1) * R] = contract(
                kept, pick, ((1,), (0,)), precision=lax.Precision.HIGHEST
            )
    for d in range(tp):
        parts_ref[d] = flat_ref[d * tok : (d + 1) * tok, :]
    landed_ref[me] = parts_ref[me]

    def push(k, source, target, sent, came):
        return pltpu.make_async_remote_copy(
            src_ref=source,
            dst_ref=target.at[me],
            send_sem=sent.at[k],
            recv_sem=came.at[me],
            device_id={"tp": lax.rem(me + k, tp)},
            device_id_type=pl.DeviceIdType.MESH,
        )

    def arrival(k, target, sent, came):
        origin = lax.rem(me + k, tp)
        return pltpu.make_async_remote_copy(
            src_ref=target.at[origin],
            dst_ref=target.at[origin],
            send_sem=sent.at[k],
            recv_sem=came.at[origin],
            device_id={"tp": origin},
            device_id_type=pl.DeviceIdType.MESH,
        )

    def each(body):
        def step(k, carry):
            body(k)
            return carry

        lax.fori_loop(1, tp, step, 0)

    def parts_copy(k):
        return push(k, parts_ref.at[lax.rem(me + k, tp)], landed_ref, sent_parts, came_parts)

    def rank_copy(k):
        return push(k, rank_ref.at[me], rank_ref, sent_rank, came_rank)

    pl.semaphore_wait(barrier, tp - 1)
    each(lambda k: parts_copy(k).start())
    each(lambda k: arrival(k, landed_ref, sent_parts, came_parts).wait_recv())
    own = landed_ref[0]
    for d in range(1, tp):
        own = own + landed_ref[d]
    rank_ref[me] = own
    each(lambda k: rank_copy(k).start())
    each(lambda k: parts_copy(k).wait_send())
    each(lambda k: arrival(k, rank_ref, sent_rank, came_rank).wait_recv())
    each(lambda k: rank_copy(k).wait_send())
    for d in range(tp):
        flat_ref[d * tok : (d + 1) * tok, :] = rank_ref[d]

    short_pick = pick.astype(bf16)
    total = None
    for p in range(2):
        rows = slice(p * piece, (p + 1) * piece)

        def spread(k):
            values = flat_ref[:, k * R : (k + 1) * R].astype(bf16)
            return jnp.where(match > 0, contract(values, short_pick, ((1,), (1,))), 0.0).astype(bf16)

        low, back = spread(p), spread(2 + p)
        first = got_ref[:, rows, hidden:at].reshape(tp * piece, width)
        term = contract(back, first, ((1,), (0,)))
        total = term if total is None else total + term
        first_gradient = adapter_scale * contract(back, x, ((0,), (0,)))
        out_ref[:, rows, hidden:at] = first_gradient.astype(bf16).reshape(tp, piece, width)
        second_gradient = adapter_scale * contract(low, grads_ref[p] * live, ((0,), (0,)))
        out_ref[:, rows, :hidden] = second_gradient.astype(bf16).reshape(tp, piece, hidden)
    x_ref[...] = adapter_scale * total
    for d in range(tp):
        for p in range(2):
            out_ref[d, p * piece : p * piece + tok, at:] = x_ref[
                d * tok : (d + 1) * tok, p * half : (p + 1) * half
            ].astype(bf16)


def unpack_kernel(tp, hidden, width, got_ref, base_ref, grads_ref, first_ref, second_ref):
    piece, tok, half = first_ref.shape[1], base_ref.shape[0], width // 2
    at = hidden + width
    for d in range(tp):
        for p in range(2):
            rows = slice(p * piece, (p + 1) * piece)
            second_ref[p, :, d * hidden : (d + 1) * hidden] = got_ref[d, rows, :hidden].astype(f32)
            first_ref[p, :, d * width : (d + 1) * width] = got_ref[d, rows, hidden:at].astype(f32)
            cut = slice(d * width + p * half, d * width + (p + 1) * half)
            grads_ref[:, cut] = base_ref[:, cut] + got_ref[d, p * piece : p * piece + tok, at:].astype(f32)


def shards(
    inputs,
    out_grads,
    frozen_weights,
    adapter_first,
    adapter_second,
    group_jobs,
    owner_map,
    segment_offsets,
    segment_lengths,
):
    tp = lax.axis_size("tp")
    job_count = group_jobs.shape[0]
    tokens, hidden = out_grads.shape[1:]
    tok, model = inputs.shape
    width = model // tp
    piece = adapter_first.shape[1]
    total_rows = tp * piece
    wide = hidden + width + width // 2
    sizes = (tp, hidden, width)

    packed = pl.pallas_call(
        functools.partial(pack_kernel, *sizes),
        out_shape=jax.ShapeDtypeStruct((tp, 2 * piece, wide), bf16),
        compiler_params=PARAMS,
    )(adapter_second, adapter_first, inputs)
    got = lax.all_to_all(packed, "tp", split_axis=0, concat_axis=0, tiled=True)

    positions = jnp.arange(tokens, dtype=jnp.int32)
    slot_ids = jnp.arange(job_count, dtype=jnp.int32)
    slot_of = jnp.sum((positions[:, None] >= segment_offsets[1:job_count][None, :]).astype(jnp.int32), axis=1)
    onehot = slot_of[:, None] == slot_ids[None, :]
    starts = jnp.sum(jnp.where(onehot, segment_offsets[:job_count][None, :], 0), axis=1)
    spans = jnp.sum(jnp.where(onehot, segment_lengths[None, :], 0), axis=1)
    live = (positions - starts < spans).astype(out_grads.dtype)[:, None]
    row = jnp.arange(total_rows, dtype=jnp.int32)
    entries = jnp.arange(tp, dtype=jnp.int32)
    entry = jnp.sum(jnp.where(owner_map[None, :] == (row // piece)[:, None], entries[None, :], 0), axis=1)
    row_slot = jnp.sum(
        jnp.where(group_jobs[None, :] == (entry // SPLIT)[:, None], slot_ids[None, :], 0), axis=1
    )
    rank = (entry % SPLIT) * piece + row % piece
    match = (slot_of[:, None] == row_slot[None, :]).astype(f32)
    pick = (rank[:, None] == jnp.arange(R, dtype=jnp.int32)[None, :]).astype(f32)

    masked = out_grads * live[None]
    frozen_product = jnp.einsum("ptf,pfd->td", masked, frozen_weights, preferred_element_type=f32)
    frozen_rows = lax.psum_scatter(frozen_product, "tp", scatter_dimension=0, tiled=True)

    outgoing = pl.pallas_call(
        functools.partial(middle_kernel, *sizes, piece, tok),
        out_shape=jax.ShapeDtypeStruct((tp, 2 * piece, wide), bf16),
        scratch_shapes=[
            pltpu.VMEM((tokens, width), f32),
            pltpu.VMEM((tokens, 4 * R), f32),
            pltpu.VMEM((tp, tok, 4 * R), f32),
            pltpu.VMEM((tp, tok, 4 * R), f32),
            pltpu.VMEM((tp, tok, 4 * R), f32),
            pltpu.SemaphoreType.DMA((tp,)),
            pltpu.SemaphoreType.DMA((tp,)),
            pltpu.SemaphoreType.DMA((tp,)),
            pltpu.SemaphoreType.DMA((tp,)),
        ],
        compiler_params=pltpu.CompilerParams(
            vmem_limit_bytes=48 * 1024 * 1024, collective_id=0, has_side_effects=True
        ),
    )(got, out_grads, live, match, pick)
    returned = lax.all_to_all(outgoing, "tp", split_axis=0, concat_axis=0, tiled=True)
    return pl.pallas_call(
        functools.partial(unpack_kernel, *sizes),
        out_shape=(
            jax.ShapeDtypeStruct((tok, model), f32),
            jax.ShapeDtypeStruct((2, piece, model), f32),
            jax.ShapeDtypeStruct((2, piece, tp * hidden), f32),
        ),
        compiler_params=PARAMS,
    )(returned, frozen_rows)


def solution(mesh):
    return jax.shard_map(
        shards,
        mesh=mesh,
        in_specs=(
            P(("parts", "tp"), None),
            P(None, "parts", "tp"),
            P(None, "tp", None),
            P(None, ("parts", "tp"), None),
            P(None, ("parts", "tp"), None),
            P("parts"),
            P("parts"),
            P("parts"),
            P("parts"),
        ),
        out_specs=(
            P(("parts", "tp"), None),
            P(None, ("parts", "tp"), None),
            P(None, ("parts", "tp"), None),
        ),
        check_vma=False,
    )
```

```python
import functools

import jax
import jax.numpy as jnp
from jax import lax
from jax.experimental import pallas as pl
from jax.experimental.pallas import tpu as pltpu
from jax.sharding import PartitionSpec as P

R = 64
SPLIT = 4
adapter_scale = 0.5
PARAMS = pltpu.CompilerParams(vmem_limit_bytes=48 * 1024 * 1024)
f32 = jnp.float32
bf16 = jnp.bfloat16


def pack_kernel(tp, hidden, width, second_ref, first_ref, inputs_ref, out_ref):
    piece, tok, half = first_ref.shape[1], inputs_ref.shape[0], width // 2
    at = hidden + width
    for d in range(tp):
        for p in range(2):
            rows = slice(p * piece, (p + 1) * piece)
            out_ref[d, rows, :hidden] = second_ref[p, :, d * hidden : (d + 1) * hidden]
            out_ref[d, rows, hidden:at] = first_ref[p, :, d * width : (d + 1) * width]
            start = d * width + p * half
            out_ref[d, p * piece : p * piece + tok, at:] = inputs_ref[:, start : start + half]


def contract(a, b, dims, precision=None):
    return lax.dot_general(a, b, (dims, ((), ())), precision=precision, preferred_element_type=f32)


def middle_kernel(
    tp, hidden, width, piece, tok, got_ref, grads_ref, live_ref, match_ref, pick_ref, out_ref,
    x_ref, flat_ref, parts_ref, landed_ref, rank_ref, sent_parts, came_parts, sent_rank, came_rank,
):
    half, at = width // 2, hidden + width
    me = lax.axis_index("tp")

    barrier = pltpu.get_barrier_semaphore()

    def greet(k, carry):
        pl.semaphore_signal(
            barrier, inc=1, device_id={"tp": lax.rem(me + k, tp)}, device_id_type=pl.DeviceIdType.MESH
        )
        return carry

    lax.fori_loop(1, tp, greet, 0)

    for d in range(tp):
        for p in range(2):
            x_ref[d * tok : (d + 1) * tok, p * half : (p + 1) * half] = got_ref[
                d, p * piece : p * piece + tok, at:
            ].astype(f32)
    x = x_ref[...].astype(bf16)
    match = match_ref[...]
    pick = pick_ref[...]
    live = live_ref[...]
    for p in range(2):
        rows = slice(p * piece, (p + 1) * piece)
        first = got_ref[:, rows, hidden:at].reshape(tp * piece, width)
        second = got_ref[:, rows, :hidden].reshape(tp * piece, hidden)
        low = contract(x, first, ((1,), (1,)))
        back = contract(grads_ref[p] * live, second, ((1,), (1,)))
        for k, value in ((p, low), (2 + p, back)):
            kept = jnp.where(match > 0, value, 0.0)
            flat_ref[:, k * R : (k + 1) * R] = contract(
                kept, pick, ((1,), (0,)), precision=lax.Precision.HIGHEST
            )
    for d in range(tp):
        parts_ref[d] = flat_ref[d * tok : (d + 1) * tok, :]
    landed_ref[me] = parts_ref[me]

    def push(k, source, target, sent, came):
        return pltpu.make_async_remote_copy(
            src_ref=source,
            dst_ref=target.at[me],
            send_sem=sent.at[k],
            recv_sem=came.at[me],
            device_id={"tp": lax.rem(me + k, tp)},
            device_id_type=pl.DeviceIdType.MESH,
        )

    def arrival(k, target, sent, came):
        origin = lax.rem(me + k, tp)
        return pltpu.make_async_remote_copy(
            src_ref=target.at[origin],
            dst_ref=target.at[origin],
            send_sem=sent.at[k],
            recv_sem=came.at[origin],
            device_id={"tp": origin},
            device_id_type=pl.DeviceIdType.MESH,
        )

    def each(body):
        def step(k, carry):
            body(k)
            return carry

        lax.fori_loop(1, tp, step, 0)

    def parts_copy(k):
        return push(k, parts_ref.at[lax.rem(me + k, tp)], landed_ref, sent_parts, came_parts)

    def rank_copy(k):
        return push(k, rank_ref.at[me], rank_ref, sent_rank, came_rank)

    pl.semaphore_wait(barrier, tp - 1)
    each(lambda k: parts_copy(k).start())
    each(lambda k: arrival(k, landed_ref, sent_parts, came_parts).wait_recv())
    own = landed_ref[0]
    for d in range(1, tp):
        own = own + landed_ref[d]
    rank_ref[me] = own
    each(lambda k: rank_copy(k).start())
    each(lambda k: parts_copy(k).wait_send())
    each(lambda k: arrival(k, rank_ref, sent_rank, came_rank).wait_recv())
    each(lambda k: rank_copy(k).wait_send())
    for d in range(tp):
        flat_ref[d * tok : (d + 1) * tok, :] = rank_ref[d]

    short_pick = pick.astype(bf16)
    total = None
    for p in range(2):
        rows = slice(p * piece, (p + 1) * piece)

        def spread(k):
            values = flat_ref[:, k * R : (k + 1) * R].astype(bf16)
            return jnp.where(match > 0, contract(values, short_pick, ((1,), (1,))), 0.0).astype(bf16)

        low, back = spread(p), spread(2 + p)
        first = got_ref[:, rows, hidden:at].reshape(tp * piece, width)
        term = contract(back, first, ((1,), (0,)))
        total = term if total is None else total + term
        first_gradient = adapter_scale * contract(back, x, ((0,), (0,)))
        out_ref[:, rows, hidden:at] = first_gradient.astype(bf16).reshape(tp, piece, width)
        second_gradient = adapter_scale * contract(low, grads_ref[p] * live, ((0,), (0,)))
        out_ref[:, rows, :hidden] = second_gradient.astype(bf16).reshape(tp, piece, hidden)
    x_ref[...] = adapter_scale * total
    for d in range(tp):
        for p in range(2):
            out_ref[d, p * piece : p * piece + tok, at:] = x_ref[
                d * tok : (d + 1) * tok, p * half : (p + 1) * half
            ].astype(bf16)


def unpack_kernel(tp, hidden, width, got_ref, base_ref, grads_ref, first_ref, second_ref):
    piece, tok, half = first_ref.shape[1], base_ref.shape[0], width // 2
    at = hidden + width
    for d in range(tp):
        for p in range(2):
            rows = slice(p * piece, (p + 1) * piece)
            second_ref[p, :, d * hidden : (d + 1) * hidden] = got_ref[d, rows, :hidden].astype(f32)
            first_ref[p, :, d * width : (d + 1) * width] = got_ref[d, rows, hidden:at].astype(f32)
            cut = slice(d * width + p * half, d * width + (p + 1) * half)
            grads_ref[:, cut] = base_ref[:, cut] + got_ref[d, p * piece : p * piece + tok, at:].astype(f32)


def shards(
    inputs,
    out_grads,
    frozen_weights,
    adapter_first,
    adapter_second,
    group_jobs,
    owner_map,
    segment_offsets,
    segment_lengths,
):
    tp = lax.axis_size("tp")
    job_count = group_jobs.shape[0]
    tokens, hidden = out_grads.shape[1:]
    tok, model = inputs.shape
    width = model // tp
    piece = adapter_first.shape[1]
    total_rows = tp * piece
    wide = hidden + width + width // 2
    sizes = (tp, hidden, width)

    packed = pl.pallas_call(
        functools.partial(pack_kernel, *sizes),
        out_shape=jax.ShapeDtypeStruct((tp, 2 * piece, wide), bf16),
        compiler_params=PARAMS,
    )(adapter_second, adapter_first, inputs)
    got = lax.all_to_all(packed, "tp", split_axis=0, concat_axis=0, tiled=True)

    positions = jnp.arange(tokens, dtype=jnp.int32)
    slot_ids = jnp.arange(job_count, dtype=jnp.int32)
    slot_of = jnp.sum((positions[:, None] >= segment_offsets[1:job_count][None, :]).astype(jnp.int32), axis=1)
    onehot = slot_of[:, None] == slot_ids[None, :]
    starts = jnp.sum(jnp.where(onehot, segment_offsets[:job_count][None, :], 0), axis=1)
    spans = jnp.sum(jnp.where(onehot, segment_lengths[None, :], 0), axis=1)
    live = (positions - starts < spans).astype(out_grads.dtype)[:, None]
    row = jnp.arange(total_rows, dtype=jnp.int32)
    entries = jnp.arange(tp, dtype=jnp.int32)
    entry = jnp.sum(jnp.where(owner_map[None, :] == (row // piece)[:, None], entries[None, :], 0), axis=1)
    row_slot = jnp.sum(
        jnp.where(group_jobs[None, :] == (entry // SPLIT)[:, None], slot_ids[None, :], 0), axis=1
    )
    rank = (entry % SPLIT) * piece + row % piece
    match = (slot_of[:, None] == row_slot[None, :]).astype(f32)
    pick = (rank[:, None] == jnp.arange(R, dtype=jnp.int32)[None, :]).astype(f32)

    masked = out_grads * live[None]
    frozen_product = jnp.einsum("ptf,pfd->td", masked, frozen_weights, preferred_element_type=f32)
    core = lax.axis_index("tp") % 2
    split = frozen_product.reshape(tp // 2, 2, tok, model)
    kept = lax.dynamic_index_in_dim(split, core, 1, keepdims=False)
    given = lax.dynamic_index_in_dim(split, 1 - core, 1, keepdims=False)
    swap = [(d, d ^ 1) for d in range(tp)]
    paired = (kept + lax.ppermute(given, "tp", swap)).reshape(tokens // 2, model)
    groups = [list(range(c, tp, 2)) for c in range(2)]
    frozen_rows = lax.psum_scatter(
        paired, "tp", scatter_dimension=0, axis_index_groups=groups, tiled=True
    )

    outgoing = pl.pallas_call(
        functools.partial(middle_kernel, *sizes, piece, tok),
        out_shape=jax.ShapeDtypeStruct((tp, 2 * piece, wide), bf16),
        scratch_shapes=[
            pltpu.VMEM((tokens, width), f32),
            pltpu.VMEM((tokens, 4 * R), f32),
            pltpu.VMEM((tp, tok, 4 * R), f32),
            pltpu.VMEM((tp, tok, 4 * R), f32),
            pltpu.VMEM((tp, tok, 4 * R), f32),
            pltpu.SemaphoreType.DMA((tp,)),
            pltpu.SemaphoreType.DMA((tp,)),
            pltpu.SemaphoreType.DMA((tp,)),
            pltpu.SemaphoreType.DMA((tp,)),
        ],
        compiler_params=pltpu.CompilerParams(
            vmem_limit_bytes=48 * 1024 * 1024, collective_id=0, has_side_effects=True
        ),
    )(got, out_grads, live, match, pick)
    returned = lax.all_to_all(outgoing, "tp", split_axis=0, concat_axis=0, tiled=True)
    return pl.pallas_call(
        functools.partial(unpack_kernel, *sizes),
        out_shape=(
            jax.ShapeDtypeStruct((tok, model), f32),
            jax.ShapeDtypeStruct((2, piece, model), f32),
            jax.ShapeDtypeStruct((2, piece, tp * hidden), f32),
        ),
        compiler_params=PARAMS,
    )(returned, frozen_rows)


def solution(mesh):
    return jax.shard_map(
        shards,
        mesh=mesh,
        in_specs=(
            P(("parts", "tp"), None),
            P(None, "parts", "tp"),
            P(None, "tp", None),
            P(None, ("parts", "tp"), None),
            P(None, ("parts", "tp"), None),
            P("parts"),
            P("parts"),
            P("parts"),
            P("parts"),
        ),
        out_specs=(
            P(("parts", "tp"), None),
            P(None, ("parts", "tp"), None),
            P(None, ("parts", "tp"), None),
        ),
        check_vma=False,
    )
```
